128 devices in a mesh: sta: 4 (over y), blk: 32 (over z, x, core).
Axes of the slice: x: 4, y: 4, z: 4, core: 2. Of those that a mesh axis runs over, the one named last changes fastest.
Arguments:
- sgt_block: bfloat16 [8, 32, 3072, 1024], P('sta', 'blk'), may hold values from -6 to 6
- weights_home: bfloat16 [16384, 512], P('blk'), may hold values from -0.25 to 0.25
- weights_strad: bfloat16 [16384, 512], P('blk'), may hold values from -0.25 to 0.25
- moment: bfloat16 [16384, 6], P('blk'), may hold values from -3 to 3
- source_time: float32 [16384, 16], P('blk'), may hold values from 0.02 to 0.5
- home_pos: int32 [16384], P('blk'), may hold values from 0 to 1023, as said below
- strad_pos: int32 [16384], P('blk'), may hold values from -1 to 1023, as said below
Outputs:
- seismograms: float32 [8, 16384, 1024], P('sta', 'blk')
The draws below stay inside these ranges and needn't reach their ends.
Inputs may be any that keep to these rules, and one draw needn't show every extreme that they name: home_pos[e] // 32 names the home block and home_pos[e] % 32 a slot. The home and straddling positions of one device's events are all distinct, so no block receives more than 32 entries from one device; some block receives exactly 32 from every device. Either -1 or a position whose block strad_pos[e] // 32 is (home_pos[e] // 32 + 1) % 32.
All inputs are finite; a program needn't handle non-finite values.
Results may differ from the reference program's by a relative error of at most 0.004.
Values may be sent and summed in bfloat16 or wider, within the bound.
No kernel may reach another device: no remote copies, remote signals or barrier semaphores. Data moves between devices by JAX's collectives and lax.ppermute only.
A program may use at most 128 MiB of HBM per device.

```python
import math
import jax
import jax.numpy as jnp
from jax import lax

NT = 1024
PTS = 512
EV_DEV = 512
LSTF = 16
STATIONS = 8
EVENTS = 16384
N_BLK = 32


def pin_slot(row, rank, target, capacity):
    return ((row - row[rank] + target) % capacity).astype(jnp.int32)


def source_plan(source_key, device, hot_block):
    capacity = 2 * EV_DEV // N_BLK
    key_pair, key_strad, key_slots, key_order = jax.random.split(source_key, 4)
    blocks = jnp.arange(N_BLK, dtype=jnp.int32)
    distance = (blocks - hot_block) % N_BLK
    offset = jnp.maximum(distance - 2, 0)
    pair_shift = jax.random.randint(key_pair, (N_BLK,), -(capacity // 4), capacity // 4 + 1)
    shift_here = pair_shift[offset // 2] * jnp.where(offset % 2 == 0, 1, -1)
    home_count = jnp.where(distance == 0, capacity, jnp.where(distance == 1, 0, capacity // 2 + shift_here))
    prev_count = jnp.roll(home_count, 1)
    free_room = jnp.minimum(prev_count, capacity - home_count)
    strad_low = jnp.where(blocks == N_BLK - 1, jnp.minimum(1, free_room), 0)
    strad_count = jax.random.randint(key_strad, (N_BLK,), strad_low, free_room + 1)
    slot_order = jax.vmap(lambda subkey: jax.random.permutation(subkey, capacity))(jax.random.split(key_slots, N_BLK)).astype(jnp.int32)
    slot_order = slot_order.at[0].set(pin_slot(slot_order[0], 0, 0, capacity))
    last_rank = jnp.where(device % 2 == 0, 0, home_count[N_BLK - 1])
    slot_order = slot_order.at[N_BLK - 1].set(pin_slot(slot_order[N_BLK - 1], last_rank, capacity - 1, capacity))
    rank_in = jnp.arange(capacity, dtype=jnp.int32)
    active = rank_in[None, :] < home_count[:, None]
    home_where = blocks[:, None] * capacity + slot_order
    next_block = (blocks + 1) % N_BLK
    straddles = active & (rank_in[None, :] < strad_count[next_block][:, None])
    next_rank = jnp.minimum(home_count[next_block][:, None] + rank_in[None, :], capacity - 1)
    strad_where = next_block[:, None] * capacity + jnp.take_along_axis(slot_order[next_block], next_rank, axis=1)
    flat_active = active.reshape(-1)
    order_rank = jnp.cumsum(flat_active.astype(jnp.int32)) - 1
    event_order = jax.random.permutation(key_order, EV_DEV)
    target = jnp.where(flat_active, event_order[jnp.clip(order_rank, 0, EV_DEV - 1)], EV_DEV)
    home_pos = jnp.zeros((EV_DEV,), jnp.int32).at[target].set(home_where.reshape(-1).astype(jnp.int32), mode='drop')
    strad_value = jnp.where(straddles, strad_where, -1).reshape(-1).astype(jnp.int32)
    strad_pos = jnp.full((EV_DEV,), -1, jnp.int32).at[target].set(strad_value, mode='drop')
    return (home_pos, strad_pos)


def event_plan(base_key):
    hot_key, rest_key = jax.random.split(base_key)
    hot_block = jax.random.randint(hot_key, (), 1, N_BLK - 3)
    source_keys = jax.random.split(rest_key, N_BLK)
    devices = jnp.arange(N_BLK, dtype=jnp.int32)
    home_pos, strad_pos = jax.vmap(lambda subkey, device: source_plan(subkey, device, hot_block))(source_keys, devices)
    return (home_pos.reshape(-1), strad_pos.reshape(-1))


def draw_home_pos(key, part):
    return event_plan(key)[0]


def draw_strad_pos(key, part):
    return event_plan(key)[1]


def shard_levels(rng, dims, shards, least, high):
    loudness, own = 1.0, jax.random.fold_in(rng, 6)
    for axis_at, shards_of in shards:
        heights = jnp.exp(jax.random.uniform(jax.random.fold_in(own, axis_at), (shards_of,), jnp.float32, least / len(shards), high / len(shards)))
        loudness = loudness * jnp.repeat(heights, dims[axis_at] // shards_of).reshape([-1 if axis == axis_at else 1 for axis in range(len(dims))])
    return loudness


def bell_draw(key, extent, deviation, bound, cuts=(), kind=jnp.bfloat16):
    gain = shard_levels(key, extent, cuts, -0.22, 0.18) if cuts else 1.0
    array = jax.random.normal(key, extent, jnp.float32) * deviation * gain
    return jnp.minimum(jnp.maximum(array, -bound), bound).astype(kind)


def setup_inputs(seed: int = 0) -> dict:
    keys = jax.random.split(jax.random.key(seed), 8)
    return {
        "sgt_block": bell_draw(keys[0], (STATIONS, N_BLK, 6 * PTS, NT), 1.0, 6.0, ((0, 4), (1, 32))),
        "weights_home": bell_draw(keys[1], (EVENTS, PTS), PTS ** -0.5, 0.25, ((0, 32),)),
        "weights_strad": bell_draw(keys[2], (EVENTS, PTS), PTS ** -0.5, 0.25, ((0, 32),)),
        "moment": bell_draw(keys[3], (EVENTS, 6), 0.5, 3.0, ((0, 32),)),
        "source_time": jnp.clip(jnp.exp(math.log(0.5) - 3.218876 * jax.random.uniform(keys[4], (EVENTS, LSTF), jnp.float32) ** shard_levels(keys[4], (EVENTS, LSTF), ((0, 32),), -0.2, 0.2)), 0.02, 0.5),
        "home_pos": draw_home_pos(jax.random.fold_in(keys[7], 71), 0),
        "strad_pos": draw_strad_pos(jax.random.fold_in(keys[7], 71), 0),
    }


def combine_rows(weights, moment):
    product = weights.astype(jnp.float32)[:, None, :] * moment.astype(jnp.float32)[:, :, None]
    return product.astype(jnp.bfloat16).reshape(weights.shape[0], 6 * weights.shape[1])


def convolve(trace, source_time):
    taps = source_time.shape[1]
    length = trace.shape[-1]
    padded = jnp.pad(trace, ((0, 0), (0, 0), (taps - 1, 0)))
    result = jnp.zeros(trace.shape, jnp.float32)
    for lag in range(taps):
        start = taps - 1 - lag
        result = result + source_time[:, lag][:, None, None] * padded[:, :, start:start + length]
    return result


def reference(sgt_block, weights_home, weights_strad, moment, source_time, home_pos, strad_pos):
    capacity = 2 * EV_DEV // N_BLK
    slot_count = 2 * EV_DEV
    owner = jnp.arange(EVENTS, dtype=jnp.int32) // EV_DEV
    home_flat = (owner * slot_count + home_pos).astype(jnp.int32)
    strad_flat = jnp.where(strad_pos >= 0, owner * slot_count + strad_pos, N_BLK * slot_count).astype(jnp.int32)
    slot_rows = jnp.zeros((N_BLK * slot_count, 6 * PTS), jnp.bfloat16)
    slot_rows = slot_rows.at[home_flat].set(combine_rows(weights_home, moment))
    slot_rows = slot_rows.at[strad_flat].set(combine_rows(weights_strad, moment), mode="drop")
    slot_rows = slot_rows.reshape(N_BLK, N_BLK, capacity, 6 * PTS)

    def one_block(block):
        block_rows = jnp.take(slot_rows, block, axis=1).reshape(N_BLK * capacity, 6 * PTS).astype(jnp.float32)
        volume = jnp.take(sgt_block, block, axis=1).astype(jnp.float32)
        return jnp.einsum("rk,skt->rst", block_rows, volume).astype(jnp.bfloat16)

    partial_value = lax.map(one_block, jnp.arange(N_BLK, dtype=jnp.int32))
    flat = partial_value.reshape(N_BLK * N_BLK * capacity, STATIONS, NT)
    home_index = ((home_pos // capacity) * (N_BLK * capacity) + owner * capacity + home_pos % capacity).astype(jnp.int32)
    strad_safe = jnp.maximum(strad_pos, 0)
    strad_index = ((strad_safe // capacity) * (N_BLK * capacity) + owner * capacity + strad_safe % capacity).astype(jnp.int32)
    straddles = (strad_pos >= 0)[:, None, None]
    trace = flat[home_index].astype(jnp.float32) + jnp.where(straddles, flat[strad_index].astype(jnp.float32), jnp.float32(0.0))
    return jnp.swapaxes(convolve(trace, source_time), 0, 1)
```

```python
import jax
import jax.numpy as jnp
from jax import lax
from jax.experimental import pallas as pl
from jax.experimental.pallas import tpu as pltpu
from jax.sharding import PartitionSpec as P

LANES = 128
PARTS = 6
EXTRA = 8
VMEM = 60 * 1024 * 1024


def contract_last(left, right):
    return lax.dot_general(left, right, (((1,), (1,)), ((), ())), preferred_element_type=jnp.float32)


def pack_kernel(capacity, home_ref, strad_ref, wh_ref, ws_ref, moment_ref, out_ref):
    step = pl.program_id(0)
    dests = out_ref.shape[0]
    slots = dests * capacity
    events, points = wh_ref.shape
    ids = lax.broadcasted_iota(jnp.int32, (slots, events), 0) + step * slots
    home = (ids == home_ref[...]).astype(jnp.float32).astype(jnp.bfloat16)
    strad = (ids == strad_ref[...]).astype(jnp.float32).astype(jnp.bfloat16)
    rows = jnp.dot(home, wh_ref[...], preferred_element_type=jnp.float32)
    rows = rows + jnp.dot(strad, ws_ref[...], preferred_element_type=jnp.float32)
    rows = rows.astype(jnp.bfloat16)
    parts = points // LANES
    for j in range(parts):
        out_ref[:, j * capacity : (j + 1) * capacity, :] = rows[:, j * LANES : (j + 1) * LANES].reshape(
            dests, capacity, LANES
        )
    wide = jnp.concatenate(
        [moment_ref[...], jnp.zeros((EXTRA - PARTS, events), jnp.bfloat16)], axis=0
    )
    across = contract_last(wide, home + strad)
    for d in range(dests):
        first = d * capacity // LANES * LANES
        shift = d * capacity % LANES
        piece = across[:, first : first + LANES]
        if shift:
            piece = pltpu.roll(piece, LANES - shift, 1)
        out_ref[d, parts * capacity :, :] = piece.astype(jnp.bfloat16)


def pack(home_row, strad_row, weights_home, weights_strad, moment, blocks):
    events, points = weights_home.shape
    capacity = 2 * events // blocks
    height = capacity * (points // LANES) + EXTRA
    dests = 8
    whole = lambda i: (0, 0)
    return pl.pallas_call(
        lambda *refs: pack_kernel(capacity, *refs),
        grid=(blocks // dests,),
        in_specs=[
            pl.BlockSpec((1, events), whole),
            pl.BlockSpec((1, events), whole),
            pl.BlockSpec((events, points), whole),
            pl.BlockSpec((events, points), whole),
            pl.BlockSpec((PARTS, events), whole),
        ],
        out_specs=pl.BlockSpec((dests, height, LANES), lambda i: (i, 0, 0)),
        out_shape=jax.ShapeDtypeStruct((blocks, height, LANES), jnp.bfloat16),
        compiler_params=pltpu.CompilerParams(vmem_limit_bytes=VMEM),
        name="pack_rows",
    )(home_row, strad_row, weights_home, weights_strad, moment)


def field_kernel(capacity, rows_ref, sgt_ref, out_ref, combined):
    sources = rows_ref.shape[0]
    points = (rows_ref.shape[1] - EXTRA) // capacity * LANES

    @pl.when((pl.program_id(0) == 0) & (pl.program_id(1) == 0))
    def _():
        pick = lax.broadcasted_iota(jnp.int32, (capacity, LANES), 0) == lax.broadcasted_iota(
            jnp.int32, (capacity, LANES), 1
        )
        pick = pick.astype(jnp.float32).astype(jnp.bfloat16)
        packed = rows_ref[:, rows_ref.shape[1] - EXTRA :, :].reshape(sources * EXTRA, LANES)
        moments = contract_last(pick, packed)
        for m in range(sources):
            for j in range(points // LANES):
                weights = rows_ref[m, j * capacity : (j + 1) * capacity, :].astype(jnp.float32)
                for c in range(PARTS):
                    scale = moments[:, m * EXTRA + c : m * EXTRA + c + 1]
                    at = c * points + j * LANES
                    combined[m * capacity : (m + 1) * capacity, at : at + LANES] = (weights * scale).astype(
                        jnp.bfloat16
                    )

    value = jnp.dot(combined[...], sgt_ref[...], preferred_element_type=jnp.float32)
    out_ref[...] = value.astype(jnp.bfloat16).reshape(out_ref.shape)


def field(rows, sgt_block, capacity):
    sources, height, _ = rows.shape
    stations, _, depth, length = sgt_block.shape
    tile = 256
    tiles = length // tile
    return pl.pallas_call(
        lambda *refs: field_kernel(capacity, *refs),
        grid=(stations, tiles),
        in_specs=[
            pl.BlockSpec((sources, height, LANES), lambda s, j: (0, 0, 0)),
            pl.BlockSpec((None, None, depth, tile), lambda s, j: (s, 0, 0, j)),
        ],
        out_specs=pl.BlockSpec((sources, capacity, tile), lambda s, j: (0, 0, s * tiles + j)),
        out_shape=jax.ShapeDtypeStruct((sources, capacity, stations * length), jnp.bfloat16),
        scratch_shapes=[pltpu.VMEM((sources * capacity, depth), jnp.bfloat16)],
        compiler_params=pltpu.CompilerParams(vmem_limit_bytes=VMEM),
        name="field_matmul",
    )(rows, sgt_block)


def shifted(pieces, count, lane):
    turned = [pltpu.roll(piece, count, 1) for piece in pieces]
    before = [jnp.zeros_like(turned[0])] + turned[:-1]
    return [jnp.where(lane < count, b, t) for b, t in zip(before, turned)]


def trace_kernel(home_ref, strad_ref, time_ref, part_ref, out_ref, chooser, trace, taps_of):
    taps, events = time_ref.shape
    slots, length = trace.shape[0] * 2, trace.shape[1]
    columns = length // LANES

    @pl.when(pl.program_id(0) == 0)
    def _():
        home = jnp.transpose(jnp.broadcast_to(home_ref[...], (LANES, events)))
        strad = jnp.transpose(jnp.broadcast_to(strad_ref[...], (LANES, events)))
        taps_of[:, :taps] = jnp.transpose(time_ref[...])
        lane = lax.broadcasted_iota(jnp.int32, (events, LANES), 1)
        for k in range(slots // LANES):
            hit = (home == lane + k * LANES) | (strad == lane + k * LANES)
            chooser[:, k * LANES : (k + 1) * LANES] = hit.astype(jnp.float32).astype(jnp.bfloat16)

    parts = part_ref[...].reshape(slots, length)
    trace[...] = jnp.dot(chooser[...], parts, preferred_element_type=jnp.float32)
    lane = lax.broadcasted_iota(jnp.int32, (8, LANES), 1)

    def rows(i, carry):
        at = pl.ds(pl.multiple_of(i * 8, 8), 8)
        pieces = [trace[at, c * LANES : (c + 1) * LANES] for c in range(columns)]
        times = taps_of[at, :]
        near = [pieces] + [shifted(pieces, b, lane) for b in range(1, 4)]
        total = None
        for a in reversed(range(taps // 4)):
            if total is not None:
                total = shifted(total, 4, lane)
            for b in range(4):
                scale = jnp.broadcast_to(times[:, 4 * a + b : 4 * a + b + 1], (8, LANES))
                terms = [scale * piece for piece in near[b]]
                total = terms if total is None else [t + u for t, u in zip(total, terms)]
        for c in range(columns):
            out_ref[at, c * LANES : (c + 1) * LANES] = total[c]
        return carry

    lax.fori_loop(0, events // 8, rows, 0)


def traces(home_row, strad_row, source_time, parts, stations):
    taps, events = source_time.shape
    sources, capacity, width = parts.shape
    length = width // stations
    return pl.pallas_call(
        trace_kernel,
        grid=(stations,),
        in_specs=[
            pl.BlockSpec((1, events), lambda s: (0, 0)),
            pl.BlockSpec((1, events), lambda s: (0, 0)),
            pl.BlockSpec((taps, events), lambda s: (0, 0)),
            pl.BlockSpec((sources, capacity, length), lambda s: (0, 0, s)),
        ],
        out_specs=pl.BlockSpec((None, events, length), lambda s: (s, 0, 0)),
        out_shape=jax.ShapeDtypeStruct((stations, events, length), jnp.float32),
        scratch_shapes=[
            pltpu.VMEM((events, sources * capacity), jnp.bfloat16),
            pltpu.VMEM((events, length), jnp.float32),
            pltpu.VMEM((events, LANES), jnp.float32),
        ],
        compiler_params=pltpu.CompilerParams(vmem_limit_bytes=VMEM),
        name="trace_convolve",
    )(home_row, strad_row, source_time, parts)


def body(sgt_block, weights_home, weights_strad, moment, source_time, home_pos, strad_pos):
    events = weights_home.shape[0]
    blocks = lax.axis_size("blk")
    capacity = 2 * events // blocks
    stations = sgt_block.shape[0]
    home_row = home_pos.reshape(1, events)
    strad_row = strad_pos.reshape(1, events)
    packed = pack(home_row, strad_row, weights_home, weights_strad, moment.T, blocks)
    rows = lax.all_to_all(packed, "blk", split_axis=0, concat_axis=0, tiled=True)
    partial_value = field(rows, sgt_block, capacity)
    returned = lax.all_to_all(partial_value, "blk", split_axis=0, concat_axis=0, tiled=True)
    return traces(home_row, strad_row, source_time.T, returned, stations)


def solution(mesh):
    placed = (
        P("sta", "blk", None, None),
        P("blk", None),
        P("blk", None),
        P("blk", None),
        P("blk", None),
        P("blk"),
        P("blk"),
    )
    return jax.shard_map(
        body, mesh=mesh, in_specs=placed, out_specs=P("sta", "blk", None), check_vma=False
    )
```

```python
import jax
import jax.numpy as jnp
from jax import lax
from jax.experimental import pallas as pl
from jax.experimental.pallas import tpu as pltpu
from jax.sharding import PartitionSpec as P

LANES = 128
PARTS = 6
EXTRA = 8
ROWS = 512
WIDTH = 256
AHEAD = 2
VMEM = 60 * 1024 * 1024


def contract_last(left, right):
    return lax.dot_general(left, right, (((1,), (1,)), ((), ())), preferred_element_type=jnp.float32)


def pack_kernel(capacity, home_ref, strad_ref, wh_ref, ws_ref, moment_ref, out_ref):
    step = pl.program_id(0)
    dests = out_ref.shape[0]
    slots = dests * capacity
    events, points = wh_ref.shape
    ids = lax.broadcasted_iota(jnp.int32, (slots, events), 0) + step * slots
    home = (ids == home_ref[...]).astype(jnp.float32).astype(jnp.bfloat16)
    strad = (ids == strad_ref[...]).astype(jnp.float32).astype(jnp.bfloat16)
    rows = jnp.dot(home, wh_ref[...], preferred_element_type=jnp.float32)
    rows = rows + jnp.dot(strad, ws_ref[...], preferred_element_type=jnp.float32)
    rows = rows.astype(jnp.bfloat16)
    parts = points // LANES
    for j in range(parts):
        out_ref[:, j * capacity : (j + 1) * capacity, :] = rows[:, j * LANES : (j + 1) * LANES].reshape(
            dests, capacity, LANES
        )
    wide = jnp.concatenate(
        [moment_ref[...], jnp.zeros((EXTRA - PARTS, events), jnp.bfloat16)], axis=0
    )
    across = contract_last(wide, home + strad)
    for d in range(dests):
        first = d * capacity // LANES * LANES
        shift = d * capacity % LANES
        piece = across[:, first : first + LANES]
        if shift:
            piece = pltpu.roll(piece, LANES - shift, 1)
        out_ref[d, parts * capacity :, :] = piece.astype(jnp.bfloat16)


def pack(home_row, strad_row, weights_home, weights_strad, moment, blocks):
    events, points = weights_home.shape
    capacity = 2 * events // blocks
    height = capacity * (points // LANES) + EXTRA
    dests = 16
    whole = lambda i: (0, 0)
    return pl.pallas_call(
        lambda *refs: pack_kernel(capacity, *refs),
        grid=(blocks // dests,),
        in_specs=[
            pl.BlockSpec((1, events), whole),
            pl.BlockSpec((1, events), whole),
            pl.BlockSpec((events, points), whole),
            pl.BlockSpec((events, points), whole),
            pl.BlockSpec((PARTS, events), whole),
        ],
        out_specs=pl.BlockSpec((dests, height, LANES), lambda i: (i, 0, 0)),
        out_shape=jax.ShapeDtypeStruct((blocks, height, LANES), jnp.bfloat16),
        compiler_params=pltpu.CompilerParams(vmem_limit_bytes=VMEM),
        name="pack_rows",
    )(home_row, strad_row, weights_home, weights_strad, moment)


def field_kernel(capacity, tiles, rows_ref, sgt_ref, out_ref, combined, field, value, loaded, saved):
    sources, height, _ = rows_ref.shape
    points = (height - EXTRA) // capacity * LANES
    slots = sources * capacity
    length = sgt_ref.shape[-1]

    def load(k, s, start, width):
        columns = pl.ds(start, width)
        return pltpu.make_async_copy(
            sgt_ref.at[s, 0, :, columns], field.at[s, :, columns], loaded.at[k]
        )

    def save(k, s, start, width):
        columns = pl.ds(s * length + start, width)
        return pltpu.make_async_copy(value.at[:, :, columns], out_ref.at[:, :, columns], saved.at[k])

    for k, tile in enumerate(tiles[:AHEAD]):
        load(k, *tile).start()
    pick = lax.broadcasted_iota(jnp.int32, (capacity, LANES), 0) == lax.broadcasted_iota(
        jnp.int32, (capacity, LANES), 1
    )
    pick = pick.astype(jnp.float32).astype(jnp.bfloat16)
    packed = rows_ref[:, height - EXTRA :, :].reshape(sources * EXTRA, LANES)
    moments = contract_last(pick, packed)
    for m in range(sources):
        for j in range(points // LANES):
            weights = rows_ref[m, j * capacity : (j + 1) * capacity, :].astype(jnp.float32)
            for c in range(PARTS):
                scale = moments[:, m * EXTRA + c : m * EXTRA + c + 1]
                at = c * points + j * LANES
                combined[m * capacity : (m + 1) * capacity, at : at + LANES] = (weights * scale).astype(
                    jnp.bfloat16
                )
    for k, (s, start, width) in enumerate(tiles):
        load(k, s, start, width).wait()
        if k + AHEAD < len(tiles):
            load(k + AHEAD, *tiles[k + AHEAD]).start()
        for m in range(0, slots, ROWS):
            part = jnp.dot(
                combined[m : m + ROWS, :], field[s, :, start : start + width], preferred_element_type=jnp.float32
            )
            value[m // capacity : (m + ROWS) // capacity, :, s * length + start : s * length + start + width] = (
                part.astype(jnp.bfloat16).reshape(ROWS // capacity, capacity, width)
            )
        save(k, s, start, width).start()
    for k, tile in enumerate(tiles):
        save(k, *tile).wait()


def field(rows, sgt_block, capacity):
    sources, height, _ = rows.shape
    stations, _, depth, length = sgt_block.shape
    width = WIDTH
    tiles = [(s, start, width) for s in range(stations) for start in range(0, length, width)]
    flops = 2 * sources * capacity * depth * stations * length
    return pl.pallas_call(
        lambda *refs: field_kernel(capacity, tiles, *refs),
        in_specs=[
            pl.BlockSpec(memory_space=pltpu.VMEM),
            pl.BlockSpec(memory_space=pl.ANY),
        ],
        out_specs=pl.BlockSpec(memory_space=pl.ANY),
        out_shape=jax.ShapeDtypeStruct((sources, capacity, stations * length), jnp.bfloat16),
        scratch_shapes=[
            pltpu.VMEM((sources * capacity, depth), jnp.bfloat16),
            pltpu.VMEM((stations, depth, length), jnp.bfloat16),
            pltpu.VMEM((sources, capacity, stations * length), jnp.bfloat16),
            pltpu.SemaphoreType.DMA((len(tiles),)),
            pltpu.SemaphoreType.DMA((len(tiles),)),
        ],
        compiler_params=pltpu.CompilerParams(vmem_limit_bytes=VMEM),
        cost_estimate=pl.CostEstimate(flops=flops, bytes_accessed=sgt_block.size * 2, transcendentals=0),
        name="field_matmul",
    )(rows, sgt_block)


STEP = 64
SPAN = 256
PIECES = 4
PITCH = 9
DEPTH = 2


def plain(taps, seq, k):
    total = taps[0] * seq(k)
    for lag in range(1, len(taps)):
        total = total + taps[lag] * seq(k - lag)
    return total


def halved(seq):
    held = {}

    def both(m):
        if m not in held:
            held[m] = seq(2 * m) + seq(2 * m + 1)
        return held[m]

    return (lambda m: seq(2 * m)), (lambda m: seq(2 * m + 1)), both


def tap_parts(taps):
    even, odd = taps[0::2], taps[1::2]
    return even, odd, [a + b for a, b in zip(even, odd)]


def leaf_taps(taps, depth):
    if depth == 0:
        return taps
    return [value for part in tap_parts(taps) for value in leaf_taps(part, depth - 1)]


def first_carry(taps, seq, depth):
    if depth == 0:
        return []
    parts, seqs = tap_parts(taps), halved(seq)
    found = [plain(parts[1], seqs[1], -1)]
    for part, sub in zip(parts, seqs):
        found += first_carry(part, sub, depth - 1)
    return found


def fast_filter(count, leaf, seq, width, depth, carry, fresh):
    if depth == 0:
        taps = leaf(count)
        return [plain(taps, seq, k) for k in range(width)]
    seqs = halved(seq)
    late = carry.pop(0)
    place = len(fresh)
    fresh.append(None)
    a, b, c = [fast_filter(count // 2, leaf, sub, width // 2, depth - 1, carry, fresh) for sub in seqs]
    fresh[place] = b[-1]
    out = []
    for m in range(width // 2):
        out.append(a[m] + (b[m - 1] if m else late))
        out.append(c[m] - a[m] - b[m])
    return out


def trace_kernel(home_ref, strad_ref, time_ref, part_ref, out_ref, chooser, parts, even, odd, after, done, whole, scales, loaded, saved):
    taps, events = time_ref.shape
    stations, _, length = out_ref.shape
    sources, capacity, _ = part_ref.shape
    slots = sources * capacity
    groups = events // LANES
    count = length // SPAN

    def load(k, s):
        columns = pl.ds(pl.multiple_of(s * length + k * SPAN, LANES), SPAN)
        return pltpu.make_async_copy(part_ref.at[:, :, columns], parts.at[k, s], loaded.at[k])

    def save(k, s):
        columns = pl.ds(pl.multiple_of(k * SPAN, LANES), SPAN)
        return pltpu.make_async_copy(done.at[k, s], out_ref.at[s, :, columns], saved.at[k])

    for k in range(count):
        for s in range(stations):
            load(k, s).start()
    home = jnp.transpose(jnp.broadcast_to(home_ref[...], (LANES, events)))
    strad = jnp.transpose(jnp.broadcast_to(strad_ref[...], (LANES, events)))
    lane = lax.broadcasted_iota(jnp.int32, (events, LANES), 1)
    for k in range(slots // LANES):
        hit = (home == lane + k * LANES) | (strad == lane + k * LANES)
        chooser[:, k * LANES : (k + 1) * LANES] = hit.astype(jnp.float32).astype(jnp.bfloat16)
    for g in range(groups):
        for s in range(stations):
            whole[:, s * groups + g, :] = time_ref[:, g * LANES : (g + 1) * LANES]
    for k, value in enumerate(leaf_taps([whole[k] for k in range(taps)], DEPTH)):
        scales[k] = value

    def gather(k, s, part, target):
        size = events // PIECES
        picked = chooser[part * size : (part + 1) * size, :]
        trace = jnp.dot(picked, parts[k, s].reshape(slots, SPAN), preferred_element_type=jnp.float32)
        for g in range(size // LANES):
            for c in range(SPAN // LANES):
                tile = trace[g * LANES : (g + 1) * LANES, c * LANES : (c + 1) * LANES]
                at = taps + c * LANES
                target[pl.ds(at * PITCH + s * groups + part * (size // LANES) + g, LANES, PITCH), :] = jnp.transpose(tile)

    def seen(ref, start):
        held = {}

        def at(k):
            if k not in held:
                held[k] = ref[pl.ds((start + taps + k) * PITCH, 8), :]
            return held[k]

        return at

    def convolve(ref, step, carry):
        carry, index, fresh = list(carry), [0], []

        def leaf(n):
            index[0] += n
            return [scales[k] for k in range(index[0] - n, index[0])]

        out = fast_filter(taps, leaf, seen(ref, step * STEP), STEP, DEPTH, carry, fresh)
        for k in range(STEP):
            after[pl.ds((step * STEP + k) * PITCH, 8), :] = out[k]
        return fresh

    def finish(k, step):
        at = step * STEP
        for s in range(stations):
            for g in range(groups):
                done[k, s, g * LANES : (g + 1) * LANES, at : at + LANES] = jnp.transpose(
                    after[pl.ds(at * PITCH + s * groups + g, LANES, PITCH), :]
                )

    def wait(k):
        for s in range(stations):
            load(k, s).wait()

    jobs = [(s, part) for s in range(stations) for part in range(PIECES)]
    steps = SPAN // STEP

    def region(k, source, target, carry):
        @pl.when(k + 1 < count)
        def _():
            wait(k + 1)

        for step in range(steps):
            carry = convolve(source, step, carry)
            for s, part in jobs[step * len(jobs) // steps : (step + 1) * len(jobs) // steps]:
                gather(jnp.minimum(k + 1, count - 1), s, part, target)
            if (step + 1) * STEP % LANES == 0:
                finish(k, ((step + 1) * STEP - LANES) // STEP)
        target[: taps * PITCH] = source[SPAN * PITCH : (SPAN + taps) * PITCH]
        for s in range(stations):
            save(k, s).start()
        return carry

    wait(0)
    for s, part in jobs:
        gather(0, s, part, even)
    even[: taps * PITCH] = jnp.zeros((taps * PITCH, LANES), jnp.float32)

    def pair(i, carry):
        carry = region(2 * i, even, odd, carry)
        return tuple(region(2 * i + 1, odd, even, carry))

    silent = first_carry([whole[k] for k in range(taps)], seen(even, 0), DEPTH)
    lax.fori_loop(0, count // 2, pair, tuple(silent))
    for k in range(count):
        for s in range(stations):
            save(k, s).wait()


def traces(home_row, strad_row, source_time, parts, stations):
    taps, events = source_time.shape
    sources, capacity, width = parts.shape
    length = width // stations
    count = length // SPAN
    row = pl.BlockSpec(memory_space=pltpu.VMEM)
    return pl.pallas_call(
        trace_kernel,
        in_specs=[row, row, row, pl.BlockSpec(memory_space=pl.ANY)],
        out_specs=pl.BlockSpec(memory_space=pl.ANY),
        out_shape=jax.ShapeDtypeStruct((stations, events, length), jnp.float32),
        scratch_shapes=[
            pltpu.VMEM((events, sources * capacity), jnp.bfloat16),
            pltpu.VMEM((count, stations, sources, capacity, SPAN), jnp.bfloat16),
            pltpu.VMEM(((taps + SPAN) * PITCH, LANES), jnp.float32),
            pltpu.VMEM(((taps + SPAN) * PITCH, LANES), jnp.float32),
            pltpu.VMEM((SPAN * PITCH, LANES), jnp.float32),
            pltpu.VMEM((count, stations, events, SPAN), jnp.float32),
            pltpu.VMEM((taps, 8, LANES), jnp.float32),
            pltpu.VMEM((taps * 3**DEPTH // 2**DEPTH, 8, LANES), jnp.float32),
            pltpu.SemaphoreType.DMA((count,)),
            pltpu.SemaphoreType.DMA((count,)),
        ],
        compiler_params=pltpu.CompilerParams(vmem_limit_bytes=VMEM),
        name="trace_convolve",
    )(home_row, strad_row, source_time, parts)


def body(sgt_block, weights_home, weights_strad, moment, source_time, home_pos, strad_pos):
    events = weights_home.shape[0]
    blocks = lax.axis_size("blk")
    capacity = 2 * events // blocks
    stations = sgt_block.shape[0]
    home_row = home_pos.reshape(1, events)
    strad_row = strad_pos.reshape(1, events)
    packed = pack(home_row, strad_row, weights_home, weights_strad, moment.T, blocks)
    rows = lax.all_to_all(packed, "blk", split_axis=0, concat_axis=0, tiled=True)
    partial_value = field(rows, sgt_block, capacity)
    returned = lax.all_to_all(partial_value, "blk", split_axis=0, concat_axis=0, tiled=True)
    return traces(home_row, strad_row, source_time.T, returned, stations)


def solution(mesh):
    placed = (
        P("sta", "blk", None, None),
        P("blk", None),
        P("blk", None),
        P("blk", None),
        P("blk", None),
        P("blk"),
        P("blk"),
    )
    return jax.shard_map(
        body, mesh=mesh, in_specs=placed, out_specs=P("sta", "blk", None), check_vma=False
    )
```

```python
import jax
import jax.numpy as jnp
from jax import lax
from jax.experimental import pallas as pl
from jax.experimental.pallas import tpu as pltpu
from jax.sharding import PartitionSpec as P

LANES = 128
PARTS = 6
EXTRA = 8
ROWS = 512
WIDTH = 512
AHEAD = 2
VMEM = 44 * 1024 * 1024
ALL_VMEM = 60 * 1024 * 1024


def contract_last(left, right):
    return lax.dot_general(left, right, (((1,), (1,)), ((), ())), preferred_element_type=jnp.float32)


def pack_kernel(capacity, home_ref, strad_ref, wh_ref, ws_ref, moment_ref, out_ref):
    step = pl.program_id(0)
    dests = out_ref.shape[0]
    slots = dests * capacity
    events, points = wh_ref.shape
    flip = lax.rem(lax.axis_index("blk"), 2) * capacity
    ids = lax.broadcasted_iota(jnp.int32, (slots, events), 0) + step * slots
    home = (ids == home_ref[...] ^ flip).astype(jnp.float32).astype(jnp.bfloat16)
    strad = (ids == strad_ref[...] ^ flip).astype(jnp.float32).astype(jnp.bfloat16)
    rows = jnp.dot(home, wh_ref[...], preferred_element_type=jnp.float32)
    rows = rows + jnp.dot(strad, ws_ref[...], preferred_element_type=jnp.float32)
    rows = rows.astype(jnp.bfloat16)
    parts = points // LANES
    for j in range(parts):
        out_ref[:, j * capacity : (j + 1) * capacity, :] = rows[:, j * LANES : (j + 1) * LANES].reshape(
            dests, capacity, LANES
        )
    wide = jnp.concatenate(
        [moment_ref[...], jnp.zeros((EXTRA - PARTS, events), jnp.bfloat16)], axis=0
    )
    across = contract_last(wide, home + strad)
    for d in range(dests):
        first = d * capacity // LANES * LANES
        shift = d * capacity % LANES
        piece = across[:, first : first + LANES]
        if shift:
            piece = pltpu.roll(piece, LANES - shift, 1)
        out_ref[d, parts * capacity :, :] = piece.astype(jnp.bfloat16)


def pack(home_row, strad_row, weights_home, weights_strad, moment, blocks):
    events, points = weights_home.shape
    capacity = 2 * events // blocks
    height = capacity * (points // LANES) + EXTRA
    dests = 16
    whole = lambda i: (0, 0)
    return pl.pallas_call(
        lambda *refs: pack_kernel(capacity, *refs),
        grid=(blocks // dests,),
        in_specs=[
            pl.BlockSpec((1, events), whole),
            pl.BlockSpec((1, events), whole),
            pl.BlockSpec((events, points), whole),
            pl.BlockSpec((events, points), whole),
            pl.BlockSpec((PARTS, events), whole),
        ],
        out_specs=pl.BlockSpec((dests, height, LANES), lambda i: (i, 0, 0)),
        out_shape=jax.ShapeDtypeStruct((blocks, height, LANES), jnp.bfloat16),
        compiler_params=pltpu.CompilerParams(vmem_limit_bytes=ALL_VMEM),
        name="pack_rows",
    )(home_row, strad_row, weights_home, weights_strad, moment)


def field_kernel(capacity, tiles, rows_ref, own_ref, other_ref, out_ref, combined, field, value, loaded, saved):
    chips, sides, height, _ = rows_ref.shape
    points = (height - EXTRA) // capacity * LANES
    slots = chips * capacity
    length = own_ref.shape[-1]

    def load(k, side, s, start, width):
        columns = pl.ds(start, width)
        source = other_ref if side else own_ref
        return pltpu.make_async_copy(
            source.at[s, 0, :, columns], field.at[side, s, :, columns], loaded.at[k]
        )

    def save(k, side, s, start, width):
        columns = pl.ds(s * length + start, width)
        return pltpu.make_async_copy(
            value.at[:, side, :, columns], out_ref.at[:, side, :, columns], saved.at[k]
        )

    for k, tile in enumerate(tiles[:AHEAD]):
        load(k, *tile).start()
    pick = lax.broadcasted_iota(jnp.int32, (capacity, LANES), 0) == lax.broadcasted_iota(
        jnp.int32, (capacity, LANES), 1
    )
    pick = pick.astype(jnp.float32).astype(jnp.bfloat16)

    def combine(side):
        packed = rows_ref[:, side, height - EXTRA :, :].reshape(chips * EXTRA, LANES)
        moments = contract_last(pick, packed)
        for m in range(chips):
            for j in range(points // LANES):
                weights = rows_ref[m, side, j * capacity : (j + 1) * capacity, :].astype(jnp.float32)
                for c in range(PARTS):
                    scale = moments[:, m * EXTRA + c : m * EXTRA + c + 1]
                    at = c * points + j * LANES
                    combined[side, m * capacity : (m + 1) * capacity, at : at + LANES] = (
                        weights * scale
                    ).astype(jnp.bfloat16)

    combine(0)
    for k, (side, s, start, width) in enumerate(tiles):
        load(k, side, s, start, width).wait()
        if k + AHEAD < len(tiles):
            load(k + AHEAD, *tiles[k + AHEAD]).start()
        if k == 1:
            combine(1)
        for m in range(0, slots, ROWS):
            part = jnp.dot(
                combined[side, m : m + ROWS, :],
                field[side, s, :, start : start + width],
                preferred_element_type=jnp.float32,
            )
            value[
                m // capacity : (m + ROWS) // capacity, side, :, s * length + start : s * length + start + width
            ] = part.astype(jnp.bfloat16).reshape(ROWS // capacity, capacity, width)
        save(k, side, s, start, width).start()
    for k, tile in enumerate(tiles):
        save(k, *tile).wait()


def field(rows, own, other, capacity):
    chips, sides, height, _ = rows.shape
    stations, _, depth, length = own.shape
    tiles = [
        (side, s, start, WIDTH)
        for side in range(sides)
        for s in range(stations)
        for start in range(0, length, WIDTH)
    ]
    flops = 2 * sides * chips * capacity * depth * stations * length
    return pl.pallas_call(
        lambda *refs: field_kernel(capacity, tiles, *refs),
        in_specs=[
            pl.BlockSpec(memory_space=pltpu.VMEM),
            pl.BlockSpec(memory_space=pl.ANY),
            pl.BlockSpec(memory_space=pl.ANY),
        ],
        out_specs=pl.BlockSpec(memory_space=pl.ANY),
        out_shape=jax.ShapeDtypeStruct((chips, sides, capacity, stations * length), jnp.bfloat16),
        scratch_shapes=[
            pltpu.VMEM((sides, chips * capacity, depth), jnp.bfloat16),
            pltpu.VMEM((sides, stations, depth, length), jnp.bfloat16),
            pltpu.VMEM((chips, sides, capacity, stations * length), jnp.bfloat16),
            pltpu.SemaphoreType.DMA((len(tiles),)),
            pltpu.SemaphoreType.DMA((len(tiles),)),
        ],
        compiler_params=pltpu.CompilerParams(vmem_limit_bytes=VMEM),
        cost_estimate=pl.CostEstimate(flops=flops, bytes_accessed=own.size * 4, transcendentals=0),
        name="field_matmul",
    )(rows, own, other)


STEP = 64
SPAN = 256
PIECES = 4
PITCH = 9
DEPTH = 2


def plain(taps, seq, k):
    total = taps[0] * seq(k)
    for lag in range(1, len(taps)):
        total = total + taps[lag] * seq(k - lag)
    return total


def halved(seq):
    held = {}

    def both(m):
        if m not in held:
            held[m] = seq(2 * m) + seq(2 * m + 1)
        return held[m]

    return (lambda m: seq(2 * m)), (lambda m: seq(2 * m + 1)), both


def tap_parts(taps):
    even, odd = taps[0::2], taps[1::2]
    return even, odd, [a + b for a, b in zip(even, odd)]


def leaf_taps(taps, depth):
    if depth == 0:
        return taps
    return [value for part in tap_parts(taps) for value in leaf_taps(part, depth - 1)]


def first_carry(taps, seq, depth):
    if depth == 0:
        return []
    parts, seqs = tap_parts(taps), halved(seq)
    found = [plain(parts[1], seqs[1], -1)]
    for part, sub in zip(parts, seqs):
        found += first_carry(part, sub, depth - 1)
    return found


def fast_filter(count, leaf, seq, width, depth, carry, fresh):
    if depth == 0:
        taps = leaf(count)
        return [plain(taps, seq, k) for k in range(width)]
    seqs = halved(seq)
    late = carry.pop(0)
    place = len(fresh)
    fresh.append(None)
    a, b, c = [fast_filter(count // 2, leaf, sub, width // 2, depth - 1, carry, fresh) for sub in seqs]
    fresh[place] = b[-1]
    out = []
    for m in range(width // 2):
        out.append(a[m] + (b[m - 1] if m else late))
        out.append(c[m] - a[m] - b[m])
    return out


def trace_kernel(home_ref, strad_ref, time_ref, part_ref, out_ref, chooser, parts, even, odd, after, done, whole, scales, loaded, saved):
    taps, events = time_ref.shape
    stations, _, length = out_ref.shape
    sources, capacity, _ = part_ref.shape
    slots = sources * capacity
    groups = events // LANES
    count = length // SPAN

    def load(k, s):
        columns = pl.ds(pl.multiple_of(s * length + k * SPAN, LANES), SPAN)
        return pltpu.make_async_copy(part_ref.at[:, :, columns], parts.at[k, s], loaded.at[k])

    def save(k, s):
        columns = pl.ds(pl.multiple_of(k * SPAN, LANES), SPAN)
        return pltpu.make_async_copy(done.at[k, s], out_ref.at[s, :, columns], saved.at[k])

    for k in range(count):
        for s in range(stations):
            load(k, s).start()
    flip = lax.rem(lax.axis_index("blk"), 2) * capacity
    home = jnp.transpose(jnp.broadcast_to(home_ref[...] ^ flip, (LANES, events)))
    strad = jnp.transpose(jnp.broadcast_to(strad_ref[...] ^ flip, (LANES, events)))
    lane = lax.broadcasted_iota(jnp.int32, (events, LANES), 1)
    for k in range(slots // LANES):
        hit = (home == lane + k * LANES) | (strad == lane + k * LANES)
        chooser[:, k * LANES : (k + 1) * LANES] = hit.astype(jnp.float32).astype(jnp.bfloat16)
    for g in range(groups):
        for s in range(stations):
            whole[:, s * groups + g, :] = time_ref[:, g * LANES : (g + 1) * LANES]
    for k, value in enumerate(leaf_taps([whole[k] for k in range(taps)], DEPTH)):
        scales[k] = value

    def gather(k, s, part, target):
        size = events // PIECES
        picked = chooser[part * size : (part + 1) * size, :]
        trace = jnp.dot(picked, parts[k, s].reshape(slots, SPAN), preferred_element_type=jnp.float32)
        for g in range(size // LANES):
            for c in range(SPAN // LANES):
                tile = trace[g * LANES : (g + 1) * LANES, c * LANES : (c + 1) * LANES]
                at = taps + c * LANES
                target[pl.ds(at * PITCH + s * groups + part * (size // LANES) + g, LANES, PITCH), :] = jnp.transpose(tile)

    def seen(ref, start):
        held = {}

        def at(k):
            if k not in held:
                held[k] = ref[pl.ds((start + taps + k) * PITCH, 8), :]
            return held[k]

        return at

    def convolve(ref, step, carry):
        carry, index, fresh = list(carry), [0], []

        def leaf(n):
            index[0] += n
            return [scales[k] for k in range(index[0] - n, index[0])]

        out = fast_filter(taps, leaf, seen(ref, step * STEP), STEP, DEPTH, carry, fresh)
        for k in range(STEP):
            after[pl.ds((step * STEP + k) * PITCH, 8), :] = out[k]
        return fresh

    def finish(k, step):
        at = step * STEP
        for s in range(stations):
            for g in range(groups):
                done[k, s, g * LANES : (g + 1) * LANES, at : at + LANES] = jnp.transpose(
                    after[pl.ds(at * PITCH + s * groups + g, LANES, PITCH), :]
                )

    def wait(k):
        for s in range(stations):
            load(k, s).wait()

    jobs = [(s, part) for s in range(stations) for part in range(PIECES)]
    steps = SPAN // STEP

    def region(k, source, target, carry):
        @pl.when(k + 1 < count)
        def _():
            wait(k + 1)

        for step in range(steps):
            carry = convolve(source, step, carry)
            for s, part in jobs[step * len(jobs) // steps : (step + 1) * len(jobs) // steps]:
                gather(jnp.minimum(k + 1, count - 1), s, part, target)
            if (step + 1) * STEP % LANES == 0:
                finish(k, ((step + 1) * STEP - LANES) // STEP)
        target[: taps * PITCH] = source[SPAN * PITCH : (SPAN + taps) * PITCH]
        for s in range(stations):
            save(k, s).start()
        return carry

    wait(0)
    for s, part in jobs:
        gather(0, s, part, even)
    even[: taps * PITCH] = jnp.zeros((taps * PITCH, LANES), jnp.float32)

    def pair(i, carry):
        carry = region(2 * i, even, odd, carry)
        return tuple(region(2 * i + 1, odd, even, carry))

    silent = first_carry([whole[k] for k in range(taps)], seen(even, 0), DEPTH)
    lax.fori_loop(0, count // 2, pair, tuple(silent))
    for k in range(count):
        for s in range(stations):
            save(k, s).wait()


def traces(home_row, strad_row, source_time, parts, stations):
    taps, events = source_time.shape
    sources, capacity, width = parts.shape
    length = width // stations
    count = length // SPAN
    row = pl.BlockSpec(memory_space=pltpu.VMEM)
    return pl.pallas_call(
        trace_kernel,
        in_specs=[row, row, row, pl.BlockSpec(memory_space=pl.ANY)],
        out_specs=pl.BlockSpec(memory_space=pl.ANY),
        out_shape=jax.ShapeDtypeStruct((stations, events, length), jnp.float32),
        scratch_shapes=[
            pltpu.VMEM((events, sources * capacity), jnp.bfloat16),
            pltpu.VMEM((count, stations, sources, capacity, SPAN), jnp.bfloat16),
            pltpu.VMEM(((taps + SPAN) * PITCH, LANES), jnp.float32),
            pltpu.VMEM(((taps + SPAN) * PITCH, LANES), jnp.float32),
            pltpu.VMEM((SPAN * PITCH, LANES), jnp.float32),
            pltpu.VMEM((count, stations, events, SPAN), jnp.float32),
            pltpu.VMEM((taps, 8, LANES), jnp.float32),
            pltpu.VMEM((taps * 3**DEPTH // 2**DEPTH, 8, LANES), jnp.float32),
            pltpu.SemaphoreType.DMA((count,)),
            pltpu.SemaphoreType.DMA((count,)),
        ],
        compiler_params=pltpu.CompilerParams(vmem_limit_bytes=VMEM),
        name="trace_convolve",
    )(home_row, strad_row, source_time, parts)


def body(sgt_block, weights_home, weights_strad, moment, source_time, home_pos, strad_pos):
    events = weights_home.shape[0]
    blocks = lax.axis_size("blk")
    chips = blocks // 2
    capacity = 2 * events // blocks
    stations = sgt_block.shape[0]
    home_row = home_pos.reshape(1, events)
    strad_row = strad_pos.reshape(1, events)
    same_core = [[2 * k + core for k in range(chips)] for core in range(2)]

    def exchange(value):
        return lax.all_to_all(
            value, "blk", split_axis=0, concat_axis=0, tiled=True, axis_index_groups=same_core
        )

    other = lax.ppermute(sgt_block, "blk", [(i, i ^ 1) for i in range(blocks)])
    packed = pack(home_row, strad_row, weights_home, weights_strad, moment.T, blocks)
    rows = exchange(packed.reshape((chips, 2) + packed.shape[1:]))
    returned = exchange(field(rows, sgt_block, other, capacity))
    returned = returned.reshape(blocks, capacity, returned.shape[-1])
    return traces(home_row, strad_row, source_time.T, returned, stations)


def solution(mesh):
    placed = (
        P("sta", "blk", None, None),
        P("blk", None),
        P("blk", None),
        P("blk", None),
        P("blk", None),
        P("blk"),
        P("blk"),
    )
    return jax.shard_map(
        body, mesh=mesh, in_specs=placed, out_specs=P("sta", "blk", None), check_vma=False
    )
```

```python
import jax
import jax.numpy as jnp
from jax import lax
from jax.experimental import pallas as pl
from jax.experimental.pallas import tpu as pltpu
from jax.sharding import PartitionSpec as P

LANES = 128
PARTS = 6
EXTRA = 8
ROWS = 512
WIDTH = 512
AHEAD = 2
VMEM = 44 * 1024 * 1024
ALL_VMEM = 60 * 1024 * 1024


def contract_last(left, right):
    return lax.dot_general(left, right, (((1,), (1,)), ((), ())), preferred_element_type=jnp.float32)


def pack_kernel(capacity, home_ref, strad_ref, wh_ref, ws_ref, moment_ref, out_ref):
    step = pl.program_id(0)
    dests = out_ref.shape[0]
    slots = dests * capacity
    events, points = wh_ref.shape
    flip = lax.rem(lax.axis_index("blk"), 2) * capacity
    ids = lax.broadcasted_iota(jnp.int32, (slots, events), 0) + step * slots
    home = (ids == home_ref[...] ^ flip).astype(jnp.float32).astype(jnp.bfloat16)
    strad = (ids == strad_ref[...] ^ flip).astype(jnp.float32).astype(jnp.bfloat16)
    rows = jnp.dot(home, wh_ref[...], preferred_element_type=jnp.float32)
    rows = rows + jnp.dot(strad, ws_ref[...], preferred_element_type=jnp.float32)
    rows = rows.astype(jnp.bfloat16)
    parts = points // LANES
    for j in range(parts):
        out_ref[:, j * capacity : (j + 1) * capacity, :] = rows[:, j * LANES : (j + 1) * LANES].reshape(
            dests, capacity, LANES
        )
    wide = jnp.concatenate(
        [moment_ref[...], jnp.zeros((EXTRA - PARTS, events), jnp.bfloat16)], axis=0
    )
    across = contract_last(wide, home + strad)
    for d in range(dests):
        first = d * capacity // LANES * LANES
        shift = d * capacity % LANES
        piece = across[:, first : first + LANES]
        if shift:
            piece = pltpu.roll(piece, LANES - shift, 1)
        out_ref[d, parts * capacity :, :] = piece.astype(jnp.bfloat16)


def pack(home_row, strad_row, weights_home, weights_strad, moment, blocks):
    events, points = weights_home.shape
    capacity = 2 * events // blocks
    height = capacity * (points // LANES) + EXTRA
    dests = 16
    whole = lambda i: (0, 0)
    return pl.pallas_call(
        lambda *refs: pack_kernel(capacity, *refs),
        grid=(blocks // dests,),
        in_specs=[
            pl.BlockSpec((1, events), whole),
            pl.BlockSpec((1, events), whole),
            pl.BlockSpec((events, points), whole),
            pl.BlockSpec((events, points), whole),
            pl.BlockSpec((PARTS, events), whole),
        ],
        out_specs=pl.BlockSpec((dests, height, LANES), lambda i: (i, 0, 0)),
        out_shape=jax.ShapeDtypeStruct((blocks, height, LANES), jnp.bfloat16),
        compiler_params=pltpu.CompilerParams(vmem_limit_bytes=ALL_VMEM),
        name="pack_rows",
    )(home_row, strad_row, weights_home, weights_strad, moment)


def field_kernel(
    capacity, tiles, rows_ref, own_ref, other_ref, home_ref, strad_ref, time_ref,
    out_ref, chooser, scales, combined, field, loaded,
):
    chips, sides, height, _ = rows_ref.shape
    points = (height - EXTRA) // capacity * LANES
    slots = chips * capacity
    length = own_ref.shape[-1]

    def load(k, side, s, start, width):
        columns = pl.ds(start, width)
        source = other_ref if side else own_ref
        return pltpu.make_async_copy(
            source.at[s, 0, :, columns], field.at[side, s, :, columns], loaded.at[k]
        )

    for k, tile in enumerate(tiles[:AHEAD]):
        load(k, *tile).start()
    pick = lax.broadcasted_iota(jnp.int32, (capacity, LANES), 0) == lax.broadcasted_iota(
        jnp.int32, (capacity, LANES), 1
    )
    pick = pick.astype(jnp.float32).astype(jnp.bfloat16)

    def combine(side):
        packed = rows_ref[:, side, height - EXTRA :, :].reshape(chips * EXTRA, LANES)
        moments = contract_last(pick, packed)
        for m in range(chips):
            for j in range(points // LANES):
                weights = rows_ref[m, side, j * capacity : (j + 1) * capacity, :].astype(jnp.float32)
                for c in range(PARTS):
                    scale = moments[:, m * EXTRA + c : m * EXTRA + c + 1]
                    at = c * points + j * LANES
                    combined[side, m * capacity : (m + 1) * capacity, at : at + LANES] = (
                        weights * scale
                    ).astype(jnp.bfloat16)

    events = time_ref.shape[1]
    groups = events // LANES
    stations = own_ref.shape[0]
    flip = lax.rem(lax.axis_index("blk"), 2) * capacity

    def choose(first, last):
        home = jnp.transpose(jnp.broadcast_to(home_ref[...] ^ flip, (LANES, events)))
        strad = jnp.transpose(jnp.broadcast_to(strad_ref[...] ^ flip, (LANES, events)))
        lane = lax.broadcasted_iota(jnp.int32, (events, LANES), 1)
        for k in range(first, last):
            hit = (home == lane + k * LANES) | (strad == lane + k * LANES)
            chooser[:, k * LANES : (k + 1) * LANES] = hit.astype(jnp.float32).astype(jnp.bfloat16)

    def spread_taps():
        taps = [
            jnp.concatenate(
                [time_ref[k : k + 1, g * LANES : (g + 1) * LANES] for g in range(groups)] * stations, axis=0
            )
            for k in range(time_ref.shape[0])
        ]
        for k, leaf in enumerate(leaf_taps(taps, DEPTH)):
            scales[k] = leaf

    combine(0)
    for k, (side, s, start, width) in enumerate(tiles):
        load(k, side, s, start, width).wait()
        if k + AHEAD < len(tiles):
            load(k + AHEAD, *tiles[k + AHEAD]).start()
        if k == 1:
            combine(1)
        if 2 <= k < 6:
            pieces = chooser.shape[1] // LANES
            choose((k - 2) * pieces // 4, (k - 1) * pieces // 4)
        if k == 6:
            spread_taps()
        for m in range(0, slots, ROWS):
            part = jnp.dot(
                combined[side, m : m + ROWS, :],
                field[side, s, :, start : start + width],
                preferred_element_type=jnp.float32,
            )
            out_ref[
                m // capacity : (m + ROWS) // capacity, side, :, s * length + start : s * length + start + width
            ] = part.astype(jnp.bfloat16).reshape(ROWS // capacity, capacity, width)


def field(rows, own, other, home_row, strad_row, source_time, capacity):
    chips, sides, height, _ = rows.shape
    stations, _, depth, length = own.shape
    taps, events = source_time.shape
    tiles = [
        (side, s, start, WIDTH)
        for side in range(sides)
        for s in range(stations)
        for start in range(0, length, WIDTH)
    ]
    flops = 2 * sides * chips * capacity * depth * stations * length
    return pl.pallas_call(
        lambda *refs: field_kernel(capacity, tiles, *refs),
        in_specs=[
            pl.BlockSpec(memory_space=pltpu.VMEM),
            pl.BlockSpec(memory_space=pl.ANY),
            pl.BlockSpec(memory_space=pl.ANY),
            pl.BlockSpec(memory_space=pltpu.VMEM),
            pl.BlockSpec(memory_space=pltpu.VMEM),
            pl.BlockSpec(memory_space=pltpu.VMEM),
        ],
        out_specs=[pl.BlockSpec(memory_space=pltpu.VMEM)] * 3,
        out_shape=[
            jax.ShapeDtypeStruct((chips, sides, capacity, stations * length), jnp.bfloat16),
            jax.ShapeDtypeStruct((events, chips * sides * capacity), jnp.bfloat16),
            jax.ShapeDtypeStruct((taps * 3**DEPTH // 2**DEPTH, 8, LANES), jnp.float32),
        ],
        scratch_shapes=[
            pltpu.VMEM((sides, chips * capacity, depth), jnp.bfloat16),
            pltpu.VMEM((sides, stations, depth, length), jnp.bfloat16),
            pltpu.SemaphoreType.DMA((len(tiles),)),
        ],
        compiler_params=pltpu.CompilerParams(vmem_limit_bytes=VMEM),
        cost_estimate=pl.CostEstimate(flops=flops, bytes_accessed=own.size * 4, transcendentals=0),
        name="field_matmul",
    )(rows, own, other, home_row, strad_row, source_time)


STEP = 64
SPAN = 256
PIECES = 4
PITCH = 9
DEPTH = 2


def plain(taps, seq, k):
    total = taps[0] * seq(k)
    for lag in range(1, len(taps)):
        total = total + taps[lag] * seq(k - lag)
    return total


def halved(seq):
    held = {}

    def both(m):
        if m not in held:
            held[m] = seq(2 * m) + seq(2 * m + 1)
        return held[m]

    return (lambda m: seq(2 * m)), (lambda m: seq(2 * m + 1)), both


def tap_parts(taps):
    even, odd = taps[0::2], taps[1::2]
    return even, odd, [a + b for a, b in zip(even, odd)]


def leaf_taps(taps, depth):
    if depth == 0:
        return taps
    return [value for part in tap_parts(taps) for value in leaf_taps(part, depth - 1)]


def fast_filter(count, leaf, seq, width, depth, carry, fresh):
    if depth == 0:
        taps = leaf(count)
        return [plain(taps, seq, k) for k in range(width)]
    seqs = halved(seq)
    late = carry.pop(0)
    place = len(fresh)
    fresh.append(None)
    a, b, c = [fast_filter(count // 2, leaf, sub, width // 2, depth - 1, carry, fresh) for sub in seqs]
    fresh[place] = b[-1]
    out = []
    for m in range(width // 2):
        out.append(a[m] + (b[m - 1] if m else late))
        out.append(c[m] - a[m] - b[m])
    return out


def trace_kernel(taps, chooser, scales, part_ref, out_ref, even, odd, after, done, saved):
    events = chooser.shape[0]
    stations, _, length = out_ref.shape
    sources, capacity, _ = part_ref.shape
    slots = sources * capacity
    groups = events // LANES
    count = length // SPAN

    def save(k, s):
        columns = pl.ds(pl.multiple_of(k * SPAN, LANES), SPAN)
        return pltpu.make_async_copy(done.at[k, s], out_ref.at[s, :, columns], saved.at[k])

    def gather(k, s, part, target):
        size = events // PIECES
        picked = chooser[part * size : (part + 1) * size, :]
        columns = pl.ds(pl.multiple_of(s * length + k * SPAN, LANES), SPAN)
        values = part_ref[:, :, columns].reshape(slots, SPAN)
        trace = jnp.dot(picked, values, preferred_element_type=jnp.float32)
        for g in range(size // LANES):
            for c in range(SPAN // LANES):
                tile = trace[g * LANES : (g + 1) * LANES, c * LANES : (c + 1) * LANES]
                at = taps + c * LANES
                target[pl.ds(at * PITCH + s * groups + part * (size // LANES) + g, LANES, PITCH), :] = jnp.transpose(tile)

    def seen(ref, start):
        held = {}

        def at(k):
            if k not in held:
                held[k] = ref[pl.ds((start + taps + k) * PITCH, 8), :]
            return held[k]

        return at

    def convolve(ref, step, carry):
        carry, index, fresh = list(carry), [0], []

        def leaf(n):
            index[0] += n
            return [scales[k] for k in range(index[0] - n, index[0])]

        out = fast_filter(taps, leaf, seen(ref, step * STEP), STEP, DEPTH, carry, fresh)
        for k in range(STEP):
            after[pl.ds((step * STEP + k) * PITCH, 8), :] = out[k]
        return fresh

    def finish(k, step):
        at = step * STEP
        for s in range(stations):
            for g in range(groups):
                done[k, s, g * LANES : (g + 1) * LANES, at : at + LANES] = jnp.transpose(
                    after[pl.ds(at * PITCH + s * groups + g, LANES, PITCH), :]
                )

    jobs = [(s, part) for s in range(stations) for part in range(PIECES)]
    steps = SPAN // STEP

    def region(k, source, target, carry):
        for step in range(steps):
            carry = convolve(source, step, carry)
            for s, part in jobs[step * len(jobs) // steps : (step + 1) * len(jobs) // steps]:
                gather(jnp.minimum(k + 1, count - 1), s, part, target)
            if (step + 1) * STEP % LANES == 0:
                finish(k, ((step + 1) * STEP - LANES) // STEP)
        target[: taps * PITCH] = source[SPAN * PITCH : (SPAN + taps) * PITCH]
        for s in range(stations):
            save(k, s).start()
        return carry

    for s, part in jobs:
        gather(0, s, part, even)
    even[: taps * PITCH] = jnp.zeros((taps * PITCH, LANES), jnp.float32)

    def pair(i, carry):
        carry = region(2 * i, even, odd, carry)
        return tuple(region(2 * i + 1, odd, even, carry))

    silent = jnp.zeros((8, LANES), jnp.float32)
    lax.fori_loop(0, count // 2, pair, (silent,) * ((3**DEPTH - 1) // 2))
    for k in range(count):
        for s in range(stations):
            save(k, s).wait()


def traces(chooser, scales, parts, taps, stations):
    events = chooser.shape[0]
    sources, capacity, width = parts.shape
    length = width // stations
    count = length // SPAN
    held = pl.BlockSpec(memory_space=pltpu.VMEM)
    return pl.pallas_call(
        lambda *refs: trace_kernel(taps, *refs),
        in_specs=[held, held, held],
        out_specs=pl.BlockSpec(memory_space=pl.ANY),
        out_shape=jax.ShapeDtypeStruct((stations, events, length), jnp.float32),
        scratch_shapes=[
            pltpu.VMEM(((taps + SPAN) * PITCH, LANES), jnp.float32),
            pltpu.VMEM(((taps + SPAN) * PITCH, LANES), jnp.float32),
            pltpu.VMEM((SPAN * PITCH, LANES), jnp.float32),
            pltpu.VMEM((count, stations, events, SPAN), jnp.float32),
            pltpu.SemaphoreType.DMA((count,)),
        ],
        compiler_params=pltpu.CompilerParams(vmem_limit_bytes=VMEM),
        name="trace_convolve",
    )(chooser, scales, parts)


def body(sgt_block, weights_home, weights_strad, moment, source_time, home_pos, strad_pos):
    events = weights_home.shape[0]
    blocks = lax.axis_size("blk")
    chips = blocks // 2
    capacity = 2 * events // blocks
    stations = sgt_block.shape[0]
    home_row = home_pos.reshape(1, events)
    strad_row = strad_pos.reshape(1, events)
    same_core = [[2 * k + core for k in range(chips)] for core in range(2)]

    def exchange(value):
        return lax.all_to_all(
            value, "blk", split_axis=0, concat_axis=0, tiled=True, axis_index_groups=same_core
        )

    other = lax.ppermute(sgt_block, "blk", [(i, i ^ 1) for i in range(blocks)])
    packed = pack(home_row, strad_row, weights_home, weights_strad, moment.T, blocks)
    rows = exchange(packed.reshape((chips, 2) + packed.shape[1:]))
    partial_value, chooser, scales = field(
        rows, sgt_block, other, home_row, strad_row, source_time.T, capacity
    )
    returned = exchange(partial_value)
    returned = returned.reshape(blocks, capacity, returned.shape[-1])
    return traces(chooser, scales, returned, source_time.shape[1], stations)


def solution(mesh):
    placed = (
        P("sta", "blk", None, None),
        P("blk", None),
        P("blk", None),
        P("blk", None),
        P("blk", None),
        P("blk"),
        P("blk"),
    )
    return jax.shard_map(
        body, mesh=mesh, in_specs=placed, out_specs=P("sta", "blk", None), check_vma=False
    )
```

```python
import jax
import jax.numpy as jnp
from jax import lax
from jax.experimental import pallas as pl
from jax.experimental.pallas import tpu as pltpu
from jax.sharding import PartitionSpec as P

LANES = 128
PARTS = 6
EXTRA = 8
ROWS = 512
WIDTH = 512
AHEAD = 2
VMEM = 44 * 1024 * 1024
ALL_VMEM = 60 * 1024 * 1024


def contract_last(left, right):
    return lax.dot_general(left, right, (((1,), (1,)), ((), ())), preferred_element_type=jnp.float32)


def pack_kernel(capacity, home_ref, strad_ref, wh_ref, ws_ref, moment_ref, out_ref):
    step = pl.program_id(0)
    dests = out_ref.shape[0]
    slots = dests * capacity
    events, points = wh_ref.shape
    flip = lax.rem(lax.axis_index("blk"), 2) * capacity
    ids = lax.broadcasted_iota(jnp.int32, (slots, events), 0) + step * slots
    home = (ids == home_ref[...] ^ flip).astype(jnp.float32).astype(jnp.bfloat16)
    strad = (ids == strad_ref[...] ^ flip).astype(jnp.float32).astype(jnp.bfloat16)
    rows = jnp.dot(home, wh_ref[...], preferred_element_type=jnp.float32)
    rows = rows + jnp.dot(strad, ws_ref[...], preferred_element_type=jnp.float32)
    rows = rows.astype(jnp.bfloat16)
    parts = points // LANES
    for j in range(parts):
        out_ref[:, j * capacity : (j + 1) * capacity, :] = rows[:, j * LANES : (j + 1) * LANES].reshape(
            dests, capacity, LANES
        )
    wide = jnp.concatenate(
        [moment_ref[...], jnp.zeros((EXTRA - PARTS, events), jnp.bfloat16)], axis=0
    )
    across = contract_last(wide, home + strad)
    for d in range(dests):
        first = d * capacity // LANES * LANES
        shift = d * capacity % LANES
        piece = across[:, first : first + LANES]
        if shift:
            piece = pltpu.roll(piece, LANES - shift, 1)
        out_ref[d, parts * capacity :, :] = piece.astype(jnp.bfloat16)


def pack(home_row, strad_row, weights_home, weights_strad, moment, blocks):
    events, points = weights_home.shape
    capacity = 2 * events // blocks
    height = capacity * (points // LANES) + EXTRA
    dests = 16
    whole = lambda i: (0, 0)
    return pl.pallas_call(
        lambda *refs: pack_kernel(capacity, *refs),
        grid=(blocks // dests,),
        in_specs=[
            pl.BlockSpec((1, events), whole),
            pl.BlockSpec((1, events), whole),
            pl.BlockSpec((events, points), whole),
            pl.BlockSpec((events, points), whole),
            pl.BlockSpec((PARTS, events), whole),
        ],
        out_specs=pl.BlockSpec((dests, height, LANES), lambda i: (i, 0, 0)),
        out_shape=jax.ShapeDtypeStruct((blocks, height, LANES), jnp.bfloat16),
        compiler_params=pltpu.CompilerParams(vmem_limit_bytes=ALL_VMEM),
        name="pack_rows",
    )(home_row, strad_row, weights_home, weights_strad, moment)


def field_kernel(
    capacity, tiles, rows_ref, own_ref, other_ref, home_ref, strad_ref, time_ref,
    out_ref, chooser, scales, combined, field, loaded,
):
    chips, sides, height, _ = rows_ref.shape
    points = (height - EXTRA) // capacity * LANES
    slots = chips * capacity
    length = own_ref.shape[-1]

    def load(k, side, s, start, width):
        columns = pl.ds(start, width)
        source = other_ref if side else own_ref
        return pltpu.make_async_copy(
            source.at[s, 0, :, columns], field.at[side, s, :, columns], loaded.at[k]
        )

    for k, tile in enumerate(tiles[:AHEAD]):
        load(k, *tile).start()
    pick = lax.broadcasted_iota(jnp.int32, (capacity, LANES), 0) == lax.broadcasted_iota(
        jnp.int32, (capacity, LANES), 1
    )
    pick = pick.astype(jnp.float32).astype(jnp.bfloat16)

    def combine(side):
        packed = rows_ref[:, side, height - EXTRA :, :].reshape(chips * EXTRA, LANES)
        moments = contract_last(pick, packed)
        for m in range(chips):
            for j in range(points // LANES):
                weights = rows_ref[m, side, j * capacity : (j + 1) * capacity, :].astype(jnp.float32)
                for c in range(PARTS):
                    scale = moments[:, m * EXTRA + c : m * EXTRA + c + 1]
                    at = c * points + j * LANES
                    combined[side, m * capacity : (m + 1) * capacity, at : at + LANES] = (
                        weights * scale
                    ).astype(jnp.bfloat16)

    events = time_ref.shape[1]
    groups = events // LANES
    stations = own_ref.shape[0]
    flip = lax.rem(lax.axis_index("blk"), 2) * capacity

    def choose(first, last):
        home = jnp.transpose(jnp.broadcast_to(home_ref[...] ^ flip, (LANES, events)))
        strad = jnp.transpose(jnp.broadcast_to(strad_ref[...] ^ flip, (LANES, events)))
        lane = lax.broadcasted_iota(jnp.int32, (events, LANES), 1)
        for k in range(first, last):
            hit = (home == lane + k * LANES) | (strad == lane + k * LANES)
            chooser[:, k * LANES : (k + 1) * LANES] = hit.astype(jnp.float32).astype(jnp.bfloat16)

    def spread_taps():
        taps = [
            jnp.concatenate(
                [time_ref[k : k + 1, g * LANES : (g + 1) * LANES] for g in range(groups)] * stations, axis=0
            )
            for k in range(time_ref.shape[0])
        ]
        for k, leaf in enumerate(leaf_taps(taps, DEPTH)):
            scales[k] = leaf

    combine(0)
    for k, (side, s, start, width) in enumerate(tiles):
        load(k, side, s, start, width).wait()
        if k + AHEAD < len(tiles):
            load(k + AHEAD, *tiles[k + AHEAD]).start()
        if k == 1:
            combine(1)
        if 2 <= k < 6:
            pieces = chooser.shape[1] // LANES
            choose((k - 2) * pieces // 4, (k - 1) * pieces // 4)
        if k == 6:
            spread_taps()
        for m in range(0, slots, ROWS):
            part = jnp.dot(
                combined[side, m : m + ROWS, :],
                field[side, s, :, start : start + width],
                preferred_element_type=jnp.float32,
            )
            out_ref[
                m // capacity : (m + ROWS) // capacity, side, :, s * length + start : s * length + start + width
            ] = part.astype(jnp.bfloat16).reshape(ROWS // capacity, capacity, width)


def field(rows, own, other, home_row, strad_row, source_time, capacity):
    chips, sides, height, _ = rows.shape
    stations, _, depth, length = own.shape
    taps, events = source_time.shape
    tiles = [
        (side, s, start, WIDTH)
        for side in range(sides)
        for s in range(stations)
        for start in range(0, length, WIDTH)
    ]
    flops = 2 * sides * chips * capacity * depth * stations * length
    return pl.pallas_call(
        lambda *refs: field_kernel(capacity, tiles, *refs),
        in_specs=[
            pl.BlockSpec(memory_space=pltpu.VMEM),
            pl.BlockSpec(memory_space=pl.ANY),
            pl.BlockSpec(memory_space=pl.ANY),
            pl.BlockSpec(memory_space=pltpu.VMEM),
            pl.BlockSpec(memory_space=pltpu.VMEM),
            pl.BlockSpec(memory_space=pltpu.VMEM),
        ],
        out_specs=[pl.BlockSpec(memory_space=pltpu.VMEM)] * 3,
        out_shape=[
            jax.ShapeDtypeStruct((chips, sides, capacity, stations * length), jnp.bfloat16),
            jax.ShapeDtypeStruct((events, chips * sides * capacity), jnp.bfloat16),
            jax.ShapeDtypeStruct((taps * 3**DEPTH // 2**DEPTH, 8, LANES), jnp.float32),
        ],
        scratch_shapes=[
            pltpu.VMEM((sides, chips * capacity, depth), jnp.bfloat16),
            pltpu.VMEM((sides, stations, depth, length), jnp.bfloat16),
            pltpu.SemaphoreType.DMA((len(tiles),)),
        ],
        compiler_params=pltpu.CompilerParams(vmem_limit_bytes=VMEM),
        cost_estimate=pl.CostEstimate(flops=flops, bytes_accessed=own.size * 4, transcendentals=0),
        name="field_matmul",
    )(rows, own, other, home_row, strad_row, source_time)


STEP = 64
SPAN = 256
PIECES = 4
PITCH = 9
DEPTH = 2


def plain(taps, seq, k):
    total = taps[0] * seq(k)
    for lag in range(1, len(taps)):
        total = total + taps[lag] * seq(k - lag)
    return total


def halved(seq):
    held = {}

    def both(m):
        if m not in held:
            held[m] = seq(2 * m) + seq(2 * m + 1)
        return held[m]

    return (lambda m: seq(2 * m)), (lambda m: seq(2 * m + 1)), both


def tap_parts(taps):
    even, odd = taps[0::2], taps[1::2]
    return even, odd, [a + b for a, b in zip(even, odd)]


def leaf_taps(taps, depth):
    if depth == 0:
        return taps
    return [value for part in tap_parts(taps) for value in leaf_taps(part, depth - 1)]


def fast_filter(count, leaf, seq, width, depth, carry, fresh):
    if depth == 0:
        taps = leaf(count)
        return [plain(taps, seq, k) for k in range(width)]
    seqs = halved(seq)
    late = carry.pop(0)
    place = len(fresh)
    fresh.append(None)
    a, b, c = [fast_filter(count // 2, leaf, sub, width // 2, depth - 1, carry, fresh) for sub in seqs]
    fresh[place] = b[-1]
    out = []
    for m in range(width // 2):
        out.append(a[m] + (b[m - 1] if m else late))
        out.append(c[m] - a[m] - b[m])
    return out


def trace_kernel(taps, chooser, scales, part_ref, out_ref, even, odd, after, done, saved):
    events = chooser.shape[0]
    stations, _, length = out_ref.shape
    sources, capacity, _ = part_ref.shape
    slots = sources * capacity
    groups = events // LANES
    count = length // SPAN

    def save(k, s):
        columns = pl.ds(pl.multiple_of(k * SPAN, LANES), SPAN)
        return pltpu.make_async_copy(done.at[k, s], out_ref.at[s, :, columns], saved.at[k])

    def gather(k, s, part, target):
        size = events // PIECES
        picked = chooser[part * size : (part + 1) * size, :]
        columns = pl.ds(pl.multiple_of(s * length + k * SPAN, LANES), SPAN)
        values = part_ref[:, :, columns].reshape(slots, SPAN)
        trace = jnp.dot(picked, values, preferred_element_type=jnp.float32)
        for g in range(size // LANES):
            for c in range(SPAN // LANES):
                tile = trace[g * LANES : (g + 1) * LANES, c * LANES : (c + 1) * LANES]
                at = taps + c * LANES
                target[pl.ds(at * PITCH + s * groups + part * (size // LANES) + g, LANES, PITCH), :] = jnp.transpose(tile)

    def seen(ref, start):
        held = {}

        def at(k):
            if k not in held:
                held[k] = ref[pl.ds((start + taps + k) * PITCH, 8), :]
            return held[k]

        return at

    def convolve(ref, step, carry):
        carry, index, fresh = list(carry), [0], []

        def leaf(n):
            index[0] += n
            return [scales[k] for k in range(index[0] - n, index[0])]

        out = fast_filter(taps, leaf, seen(ref, step * STEP), STEP, DEPTH, carry, fresh)
        for k in range(STEP):
            after[pl.ds((step * STEP + k) * PITCH, 8), :] = out[k]
        return fresh

    def finish(k, step):
        at = step * STEP
        for s in range(stations):
            for g in range(groups):
                done[k, s, g * LANES : (g + 1) * LANES, at : at + LANES] = jnp.transpose(
                    after[pl.ds(at * PITCH + s * groups + g, LANES, PITCH), :]
                )

    jobs = [(s, part) for s in range(stations) for part in range(PIECES)]
    steps = SPAN // STEP

    def region(k, source, target, carry):
        for step in range(steps):
            carry = convolve(source, step, carry)
            for s, part in jobs[step * len(jobs) // steps : (step + 1) * len(jobs) // steps]:
                gather(jnp.minimum(k + 1, count - 1), s, part, target)
            if (step + 1) * STEP % LANES == 0:
                finish(k, ((step + 1) * STEP - LANES) // STEP)
        target[: taps * PITCH] = source[SPAN * PITCH : (SPAN + taps) * PITCH]
        for s in range(stations):
            save(k, s).start()
        return carry

    for s, part in jobs:
        gather(0, s, part, even)
    even[: taps * PITCH] = jnp.zeros((taps * PITCH, LANES), jnp.float32)

    def pair(i, carry):
        carry = region(2 * i, even, odd, carry)
        return tuple(region(2 * i + 1, odd, even, carry))

    silent = jnp.zeros((8, LANES), jnp.float32)
    lax.fori_loop(0, count // 2, pair, (silent,) * ((3**DEPTH - 1) // 2))
    for k in range(count):
        for s in range(stations):
            save(k, s).wait()


def traces(chooser, scales, parts, taps, stations):
    events = chooser.shape[0]
    sources, capacity, width = parts.shape
    length = width // stations
    count = length // SPAN
    held = pl.BlockSpec(memory_space=pltpu.VMEM)
    return pl.pallas_call(
        lambda *refs: trace_kernel(taps, *refs),
        in_specs=[held, held, held],
        out_specs=pl.BlockSpec(memory_space=pl.ANY),
        out_shape=jax.ShapeDtypeStruct((stations, events, length), jnp.float32),
        scratch_shapes=[
            pltpu.VMEM(((taps + SPAN + 1) * PITCH, LANES), jnp.float32),
            pltpu.VMEM(((taps + SPAN + 1) * PITCH, LANES), jnp.float32),
            pltpu.VMEM(((SPAN + 1) * PITCH, LANES), jnp.float32),
            pltpu.VMEM((count, stations, events, SPAN), jnp.float32),
            pltpu.SemaphoreType.DMA((count,)),
        ],
        compiler_params=pltpu.CompilerParams(vmem_limit_bytes=VMEM),
        name="trace_convolve",
    )(chooser, scales, parts)


def body(sgt_block, weights_home, weights_strad, moment, source_time, home_pos, strad_pos):
    events = weights_home.shape[0]
    blocks = lax.axis_size("blk")
    chips = blocks // 2
    capacity = 2 * events // blocks
    stations = sgt_block.shape[0]
    home_row = home_pos.reshape(1, events)
    strad_row = strad_pos.reshape(1, events)
    same_core = [[2 * k + core for k in range(chips)] for core in range(2)]

    def exchange(value):
        return lax.all_to_all(
            value, "blk", split_axis=0, concat_axis=0, tiled=True, axis_index_groups=same_core
        )

    other = lax.ppermute(sgt_block, "blk", [(i, i ^ 1) for i in range(blocks)])
    packed = pack(home_row, strad_row, weights_home, weights_strad, moment.T, blocks)
    rows = exchange(packed.reshape((chips, 2) + packed.shape[1:]))
    partial_value, chooser, scales = field(
        rows, sgt_block, other, home_row, strad_row, source_time.T, capacity
    )
    returned = exchange(partial_value)
    returned = returned.reshape(blocks, capacity, returned.shape[-1])
    return traces(chooser, scales, returned, source_time.shape[1], stations)


def solution(mesh):
    placed = (
        P("sta", "blk", None, None),
        P("blk", None),
        P("blk", None),
        P("blk", None),
        P("blk", None),
        P("blk"),
        P("blk"),
    )
    return jax.shard_map(
        body, mesh=mesh, in_specs=placed, out_specs=P("sta", "blk", None), check_vma=False
    )
```

```python
import jax
import jax.numpy as jnp
from jax import lax
from jax.experimental import pallas as pl
from jax.experimental.pallas import tpu as pltpu
from jax.sharding import PartitionSpec as P

LANES = 128
PARTS = 6
EXTRA = 8
ROWS = 512
WIDTH = 512
AHEAD = 2
VMEM = 44 * 1024 * 1024
ALL_VMEM = 60 * 1024 * 1024


def contract_last(left, right):
    return lax.dot_general(left, right, (((1,), (1,)), ((), ())), preferred_element_type=jnp.float32)


def pack_kernel(capacity, home_ref, strad_ref, wh_ref, ws_ref, moment_ref, out_ref):
    step = pl.program_id(0)
    dests = out_ref.shape[0]
    slots = dests * capacity
    events, points = wh_ref.shape
    flip = lax.rem(lax.axis_index("blk"), 2) * capacity
    ids = lax.broadcasted_iota(jnp.int32, (slots, events), 0) + step * slots
    home = (ids == home_ref[...] ^ flip).astype(jnp.float32).astype(jnp.bfloat16)
    strad = (ids == strad_ref[...] ^ flip).astype(jnp.float32).astype(jnp.bfloat16)
    rows = jnp.dot(home, wh_ref[...], preferred_element_type=jnp.float32)
    rows = rows + jnp.dot(strad, ws_ref[...], preferred_element_type=jnp.float32)
    rows = rows.astype(jnp.bfloat16)
    parts = points // LANES
    for j in range(parts):
        out_ref[:, j * capacity : (j + 1) * capacity, :] = rows[:, j * LANES : (j + 1) * LANES].reshape(
            dests, capacity, LANES
        )
    wide = jnp.concatenate(
        [moment_ref[...], jnp.zeros((EXTRA - PARTS, events), jnp.bfloat16)], axis=0
    )
    across = contract_last(wide, home + strad)
    for d in range(dests):
        first = d * capacity // LANES * LANES
        shift = d * capacity % LANES
        piece = across[:, first : first + LANES]
        if shift:
            piece = pltpu.roll(piece, LANES - shift, 1)
        out_ref[d, parts * capacity :, :] = piece.astype(jnp.bfloat16)


def pack(home_row, strad_row, weights_home, weights_strad, moment, blocks):
    events, points = weights_home.shape
    capacity = 2 * events // blocks
    height = capacity * (points // LANES) + EXTRA
    dests = 16
    whole = lambda i: (0, 0)
    return pl.pallas_call(
        lambda *refs: pack_kernel(capacity, *refs),
        grid=(blocks // dests,),
        in_specs=[
            pl.BlockSpec((1, events), whole),
            pl.BlockSpec((1, events), whole),
            pl.BlockSpec((events, points), whole),
            pl.BlockSpec((events, points), whole),
            pl.BlockSpec((PARTS, events), whole),
        ],
        out_specs=pl.BlockSpec((dests, height, LANES), lambda i: (i, 0, 0)),
        out_shape=jax.ShapeDtypeStruct((blocks, height, LANES), jnp.bfloat16),
        compiler_params=pltpu.CompilerParams(vmem_limit_bytes=ALL_VMEM),
        name="pack_rows",
    )(home_row, strad_row, weights_home, weights_strad, moment)


def field_kernel(
    capacity, tiles, rows_ref, own_ref, other_ref, home_ref, strad_ref, time_ref,
    out_ref, chooser, scales, combined, field, loaded,
):
    chips, sides, height, _ = rows_ref.shape
    points = (height - EXTRA) // capacity * LANES
    slots = chips * capacity
    length = own_ref.shape[-1]

    def load(k, side, s, start, width):
        columns = pl.ds(start, width)
        source = other_ref if side else own_ref
        return pltpu.make_async_copy(
            source.at[s, 0, :, columns], field.at[side, s, :, columns], loaded.at[k]
        )

    for k, tile in enumerate(tiles[:AHEAD]):
        load(k, *tile).start()
    pick = lax.broadcasted_iota(jnp.int32, (capacity, LANES), 0) == lax.broadcasted_iota(
        jnp.int32, (capacity, LANES), 1
    )
    pick = pick.astype(jnp.float32).astype(jnp.bfloat16)

    def combine(side):
        packed = rows_ref[:, side, height - EXTRA :, :].reshape(chips * EXTRA, LANES)
        moments = contract_last(pick, packed)
        for m in range(chips):
            for j in range(points // LANES):
                weights = rows_ref[m, side, j * capacity : (j + 1) * capacity, :].astype(jnp.float32)
                for c in range(PARTS):
                    scale = moments[:, m * EXTRA + c : m * EXTRA + c + 1]
                    at = c * points + j * LANES
                    combined[side, m * capacity : (m + 1) * capacity, at : at + LANES] = (
                        weights * scale
                    ).astype(jnp.bfloat16)

    events = time_ref.shape[1]
    groups = events // LANES
    stations = own_ref.shape[0]
    flip = lax.rem(lax.axis_index("blk"), 2) * capacity

    def choose(first, last):
        home = jnp.transpose(jnp.broadcast_to(home_ref[...] ^ flip, (LANES, events)))
        strad = jnp.transpose(jnp.broadcast_to(strad_ref[...] ^ flip, (LANES, events)))
        lane = lax.broadcasted_iota(jnp.int32, (events, LANES), 1)
        for k in range(first, last):
            hit = (home == lane + k * LANES) | (strad == lane + k * LANES)
            chooser[:, k * LANES : (k + 1) * LANES] = hit.astype(jnp.float32).astype(jnp.bfloat16)

    def spread_taps():
        taps = [
            jnp.concatenate(
                [time_ref[k : k + 1, g * LANES : (g + 1) * LANES] for g in range(groups)] * stations, axis=0
            )
            for k in range(time_ref.shape[0])
        ]
        for k, leaf in enumerate(leaf_taps(taps, DEPTH)):
            scales[k] = leaf

    combine(0)
    for k, (side, s, start, width) in enumerate(tiles):
        load(k, side, s, start, width).wait()
        if k + AHEAD < len(tiles):
            load(k + AHEAD, *tiles[k + AHEAD]).start()
        if k == 1:
            combine(1)
        if 2 <= k < 6:
            pieces = chooser.shape[1] // LANES
            choose((k - 2) * pieces // 4, (k - 1) * pieces // 4)
        if k == 6:
            spread_taps()
        for m in range(0, slots, ROWS):
            part = jnp.dot(
                combined[side, m : m + ROWS, :],
                field[side, s, :, start : start + width],
                preferred_element_type=jnp.float32,
            )
            out_ref[
                m // capacity : (m + ROWS) // capacity, side, :, s * length + start : s * length + start + width
            ] = part.astype(jnp.bfloat16).reshape(ROWS // capacity, capacity, width)


def field(rows, own, other, home_row, strad_row, source_time, capacity):
    chips, sides, height, _ = rows.shape
    stations, _, depth, length = own.shape
    taps, events = source_time.shape
    tiles = [
        (side, s, start, WIDTH)
        for side in range(sides)
        for s in range(stations)
        for start in range(0, length, WIDTH)
    ]
    flops = 2 * sides * chips * capacity * depth * stations * length
    return pl.pallas_call(
        lambda *refs: field_kernel(capacity, tiles, *refs),
        in_specs=[
            pl.BlockSpec(memory_space=pltpu.VMEM),
            pl.BlockSpec(memory_space=pl.ANY),
            pl.BlockSpec(memory_space=pl.ANY),
            pl.BlockSpec(memory_space=pltpu.VMEM),
            pl.BlockSpec(memory_space=pltpu.VMEM),
            pl.BlockSpec(memory_space=pltpu.VMEM),
        ],
        out_specs=[pl.BlockSpec(memory_space=pltpu.VMEM)] * 3,
        out_shape=[
            jax.ShapeDtypeStruct((chips, sides, capacity, stations * length), jnp.bfloat16),
            jax.ShapeDtypeStruct((events, chips * sides * capacity), jnp.bfloat16),
            jax.ShapeDtypeStruct((taps * 3**DEPTH // 2**DEPTH, 8, LANES), jnp.float32),
        ],
        scratch_shapes=[
            pltpu.VMEM((sides, chips * capacity, depth), jnp.bfloat16),
            pltpu.VMEM((sides, stations, depth, length), jnp.bfloat16),
            pltpu.SemaphoreType.DMA((len(tiles),)),
        ],
        compiler_params=pltpu.CompilerParams(vmem_limit_bytes=VMEM),
        cost_estimate=pl.CostEstimate(flops=flops, bytes_accessed=own.size * 4, transcendentals=0),
        name="field_matmul",
    )(rows, own, other, home_row, strad_row, source_time)


STEP = 64
SPAN = 256
PIECES = 2
PITCH = 9
DEPTH = 2


def plain(taps, seq, k):
    total = taps[0] * seq(k)
    for lag in range(1, len(taps)):
        total = total + taps[lag] * seq(k - lag)
    return total


def halved(seq):
    held = {}

    def both(m):
        if m not in held:
            held[m] = seq(2 * m) + seq(2 * m + 1)
        return held[m]

    return (lambda m: seq(2 * m)), (lambda m: seq(2 * m + 1)), both


def tap_parts(taps):
    even, odd = taps[0::2], taps[1::2]
    return even, odd, [a + b for a, b in zip(even, odd)]


def leaf_taps(taps, depth):
    if depth == 0:
        return taps
    return [value for part in tap_parts(taps) for value in leaf_taps(part, depth - 1)]


def fast_filter(count, leaf, seq, width, depth, carry, fresh):
    if depth == 0:
        taps = leaf(count)
        return [plain(taps, seq, k) for k in range(width)]
    seqs = halved(seq)
    late = carry.pop(0)
    place = len(fresh)
    fresh.append(None)
    a, b, c = [fast_filter(count // 2, leaf, sub, width // 2, depth - 1, carry, fresh) for sub in seqs]
    fresh[place] = b[-1]
    out = []
    for m in range(width // 2):
        out.append(a[m] + (b[m - 1] if m else late))
        out.append(c[m] - a[m] - b[m])
    return out


def trace_kernel(taps, chooser, scales, part_ref, out_ref, even, odd, after, done, saved):
    events = chooser.shape[0]
    stations, _, length = out_ref.shape
    sources, capacity, _ = part_ref.shape
    slots = sources * capacity
    groups = events // LANES
    count = length // SPAN

    def save(k, s, at):
        columns = pl.ds(pl.multiple_of(k * SPAN + at, LANES), LANES)
        return pltpu.make_async_copy(
            done.at[k, s, :, pl.ds(at, LANES)], out_ref.at[s, :, columns], saved.at[k, at // LANES]
        )

    def gather(k, s, part, target):
        size = events // PIECES
        picked = chooser[part * size : (part + 1) * size, :]
        columns = pl.ds(pl.multiple_of(s * length + k * SPAN, LANES), SPAN)
        values = part_ref[:, :, columns].reshape(slots, SPAN)
        trace = jnp.dot(picked, values, preferred_element_type=jnp.float32)
        for g in range(size // LANES):
            for c in range(SPAN // LANES):
                tile = trace[g * LANES : (g + 1) * LANES, c * LANES : (c + 1) * LANES]
                at = taps + c * LANES
                target[pl.ds(at * PITCH + s * groups + part * (size // LANES) + g, LANES, PITCH), :] = jnp.transpose(tile)

    def seen(ref, start):
        held = {}

        def at(k):
            if k not in held:
                held[k] = ref[pl.ds((start + taps + k) * PITCH, 8), :]
            return held[k]

        return at

    def convolve(ref, step, carry):
        carry, index, fresh = list(carry), [0], []

        def leaf(n):
            index[0] += n
            return [scales[k] for k in range(index[0] - n, index[0])]

        out = fast_filter(taps, leaf, seen(ref, step * STEP), STEP, DEPTH, carry, fresh)
        for k in range(STEP):
            after[pl.ds((step * STEP + k) * PITCH, 8), :] = out[k]
        return fresh

    def finish(k, step):
        at = step * STEP
        for s in range(stations):
            for g in range(groups):
                done[k, s, g * LANES : (g + 1) * LANES, at : at + LANES] = jnp.transpose(
                    after[pl.ds(at * PITCH + s * groups + g, LANES, PITCH), :]
                )
            save(k, s, at).start()

    jobs = [(s, part) for s in range(stations) for part in range(PIECES)]
    steps = SPAN // STEP

    def region(k, source, target, carry):
        for step in range(steps):
            carry = convolve(source, step, carry)
            for s, part in jobs[step * len(jobs) // steps : (step + 1) * len(jobs) // steps]:
                gather(jnp.minimum(k + 1, count - 1), s, part, target)
            if (step + 1) * STEP % LANES == 0:
                finish(k, ((step + 1) * STEP - LANES) // STEP)
        target[: taps * PITCH] = source[SPAN * PITCH : (SPAN + taps) * PITCH]
        return carry

    for s, part in jobs:
        gather(0, s, part, even)
    even[: taps * PITCH] = jnp.zeros((taps * PITCH, LANES), jnp.float32)

    def pair(i, carry):
        carry = region(2 * i, even, odd, carry)
        return tuple(region(2 * i + 1, odd, even, carry))

    silent = jnp.zeros((8, LANES), jnp.float32)
    lax.fori_loop(0, count // 2, pair, (silent,) * ((3**DEPTH - 1) // 2))
    for k in range(count):
        for s in range(stations):
            for at in range(0, SPAN, LANES):
                save(k, s, at).wait()


def traces(chooser, scales, parts, taps, stations):
    events = chooser.shape[0]
    sources, capacity, width = parts.shape
    length = width // stations
    count = length // SPAN
    held = pl.BlockSpec(memory_space=pltpu.VMEM)
    return pl.pallas_call(
        lambda *refs: trace_kernel(taps, *refs),
        in_specs=[held, held, held],
        out_specs=pl.BlockSpec(memory_space=pl.ANY),
        out_shape=jax.ShapeDtypeStruct((stations, events, length), jnp.float32),
        scratch_shapes=[
            pltpu.VMEM(((taps + SPAN + 1) * PITCH, LANES), jnp.float32),
            pltpu.VMEM(((taps + SPAN + 1) * PITCH, LANES), jnp.float32),
            pltpu.VMEM(((SPAN + 1) * PITCH, LANES), jnp.float32),
            pltpu.VMEM((count, stations, events, SPAN), jnp.float32),
            pltpu.SemaphoreType.DMA((count, SPAN // LANES)),
        ],
        compiler_params=pltpu.CompilerParams(vmem_limit_bytes=VMEM),
        name="trace_convolve",
    )(chooser, scales, parts)


def body(sgt_block, weights_home, weights_strad, moment, source_time, home_pos, strad_pos):
    events = weights_home.shape[0]
    blocks = lax.axis_size("blk")
    chips = blocks // 2
    capacity = 2 * events // blocks
    stations = sgt_block.shape[0]
    home_row = home_pos.reshape(1, events)
    strad_row = strad_pos.reshape(1, events)
    same_core = [[2 * k + core for k in range(chips)] for core in range(2)]

    def exchange(value):
        return lax.all_to_all(
            value, "blk", split_axis=0, concat_axis=0, tiled=True, axis_index_groups=same_core
        )

    other = lax.ppermute(sgt_block, "blk", [(i, i ^ 1) for i in range(blocks)])
    packed = pack(home_row, strad_row, weights_home, weights_strad, moment.T, blocks)
    rows = exchange(packed.reshape((chips, 2) + packed.shape[1:]))
    partial_value, chooser, scales = field(
        rows, sgt_block, other, home_row, strad_row, source_time.T, capacity
    )
    returned = exchange(partial_value)
    returned = returned.reshape(blocks, capacity, returned.shape[-1])
    return traces(chooser, scales, returned, source_time.shape[1], stations)


def solution(mesh):
    placed = (
        P("sta", "blk", None, None),
        P("blk", None),
        P("blk", None),
        P("blk", None),
        P("blk", None),
        P("blk"),
        P("blk"),
    )
    return jax.shard_map(
        body, mesh=mesh, in_specs=placed, out_specs=P("sta", "blk", None), check_vma=False
    )
```
